128 devices in a mesh: patch: 16 (over y, z), level: 8 (over x, core).
Axes of the slice: x: 4, y: 4, z: 4, core: 2. Of those that a mesh axis runs over, the one named last changes fastest.
Arguments:
- right_side: bfloat16 [64, 262144], P(None, ('patch', 'level')), may hold values from -6 to 6
- level_pairs: bfloat16 [10, 2048, 2, 128, 128], P(None, ('patch', 'level')), may hold values from -0.375 to 0.375
- near_blocks: bfloat16 [2048, 8, 128, 128], P(('patch', 'level')), may hold values from -0.1875 to 0.1875
- near_index: int32 [2048, 8], P(('patch', 'level')), may hold values from 0 to 47
- near_count: int32 [2048], P(('patch', 'level')), may hold values from 1 to 8, as said below
Outputs:
- solution: bfloat16 [64, 262144], P(None, ('patch', 'level'))
The draws below stay inside these ranges and needn't reach their ends.
Inputs may be any that keep to these rules, and one draw needn't show every extreme that they name: `near_index`: slots at or past a block's near_count are not used. `near_count`: on every device some block uses all of that device's most slots, and on some device that most is 8.
All inputs are finite; a program needn't handle non-finite values.
Results may differ from the reference program's by a relative error of at most 0.035.
Values may be sent and summed in bfloat16 or wider, within the bound.
No kernel may reach another device: no remote copies, remote signals or barrier semaphores. Data moves between devices by JAX's collectives and lax.ppermute only.
A program may use at most 128 MiB of HBM per device.

```python
import jax
import jax.numpy as jnp

W = 128
RHS = 64
BLK_DEV = 16
NNB = 8
LOCAL_LEVELS = 3
ITERS = 3
LEVELS = 10
NBLK = 2048
N = 262144
N_PATCH = 16
N_LEVEL = 8


def draw_near_count(key, part):
    key = jax.random.fold_in(key, 11)
    key_caps, key_top, key_base, key_pick = jax.random.split(key, 4)
    device_total = NBLK // BLK_DEV
    caps = jax.random.randint(key_caps, (device_total,), max(NNB // 4, 1), NNB + 1)
    top_device = jax.random.randint(key_top, (), 0, device_total)
    caps = jnp.where(jnp.arange(device_total) == top_device, NNB, caps)
    base = jax.random.randint(key_base, (device_total, BLK_DEV), 0, 1048576)
    counts = 1 + base % caps[:, None]
    picked = jax.random.randint(key_pick, (device_total,), 0, BLK_DEV)
    counts = jnp.where(jnp.arange(BLK_DEV)[None, :] == picked[:, None], caps[:, None], counts)
    return counts.reshape(NBLK).astype(jnp.int32)


def place_ends(result, rng, least, top_value):
    index_at = [jax.random.randint(jax.random.fold_in(rng, axis), (), 0, length) for axis, length in enumerate(result.shape)]
    longest = result.shape.index(max(result.shape))
    beside = index_at[:longest] + [(index_at[longest] + 1) % result.shape[longest]] + index_at[longest + 1:]
    return result.at[tuple(index_at)].set(least).at[tuple(beside)].set(top_value)


def block_scale(stream_key, shape, cuts, low, high):
    factor_of, own = 1.0, jax.random.fold_in(stream_key, 6)
    for position, blocks in cuts:
        steps = jnp.exp(jax.random.uniform(jax.random.fold_in(own, position), (blocks,), jnp.float32, low / len(cuts), high / len(cuts)))
        factor_of = factor_of * jnp.repeat(steps, shape[position] // blocks).reshape([-1 if axis == position else 1 for axis in range(len(shape))])
    return factor_of


def noise(key, extent, width, most, cuts=(), kind=jnp.bfloat16):
    array = width * jax.random.normal(key, extent, jnp.float32)
    if cuts:
        array = array * block_scale(key, extent, cuts, -0.22, 0.18)
    return jnp.clip(array, -most, most).astype(kind)


def setup_inputs(seed: int = 0) -> dict:
    streams_of = jax.random.split(jax.random.key(seed), 6)
    right_side = noise(streams_of[0], (RHS, N), 1.0, 6.0, ((1, 128),))
    level_pairs = noise(streams_of[1], (LEVELS, NBLK, 2, W, W), (2 * W) ** -0.5, 0.375, ((1, 128),))
    near_blocks = noise(streams_of[2], (NBLK, NNB, W, W), (W * NNB) ** -0.5, 0.1875, ((0, 128),))
    near_index = place_ends(jax.random.randint(streams_of[3], (NBLK, NNB), 0, 3 * BLK_DEV), jax.random.fold_in(streams_of[3], 1), 0, (3 * BLK_DEV) - 1).astype(jnp.int32)
    near_count = draw_near_count(jax.random.fold_in(streams_of[5], 71), 0)
    return {"right_side": right_side, "level_pairs": level_pairs, "near_blocks": near_blocks, "near_index": near_index, "near_count": near_count}


coupling = 0.4


def reference(right_side, level_pairs, near_blocks, near_index, near_count):
    block_ids = jnp.arange(NBLK, dtype=jnp.int32)
    device_ids = block_ids // BLK_DEV
    patch_ids = device_ids // N_LEVEL
    level_ids = device_ids % N_LEVEL
    thirds = near_index // BLK_DEV
    offsets = near_index % BLK_DEV
    patch_near = (patch_ids[:, None] + thirds - 1) % N_PATCH
    neighbors = ((patch_near * N_LEVEL + level_ids[:, None]) * BLK_DEV + offsets).astype(jnp.int32)
    usable = (jnp.arange(NNB, dtype=jnp.int32)[None, :] < near_count[:, None]).astype(jnp.float32)
    source = right_side.astype(jnp.float32).reshape(RHS, NBLK, W)
    current = right_side.reshape(RHS, NBLK, W)
    for sweep in range(ITERS):
        mixed = current
        for level_idx in range(LEVELS):
            if level_idx < LOCAL_LEVELS:
                stride = 2 ** level_idx
            else:
                stride = BLK_DEV * 2 ** (level_idx - LOCAL_LEVELS)
            partner = mixed[:, jnp.bitwise_xor(block_ids, stride).astype(jnp.int32)]
            factor = level_pairs[level_idx].astype(jnp.float32)
            own_term = jnp.einsum("rgw,gwv->rgv", mixed.astype(jnp.float32), factor[:, 0])
            pair_term = jnp.einsum("rgw,gwv->rgv", partner.astype(jnp.float32), factor[:, 1])
            mixed = (own_term + pair_term).astype(jnp.bfloat16)
        near = jnp.zeros((RHS, NBLK, W), jnp.float32)
        for slot in range(NNB):
            taken = current[:, neighbors[:, slot]].astype(jnp.float32) * usable[:, slot][None, :, None]
            near = near + jnp.einsum("rgw,gwv->rgv", taken, near_blocks[:, slot].astype(jnp.float32))
        current = (source - coupling * (mixed.astype(jnp.float32) + near)).astype(jnp.bfloat16)
    return current.reshape(RHS, NBLK * W)
```

```python
import functools

import jax
import jax.numpy as jnp
from jax import lax
from jax.experimental import pallas as pl
from jax.experimental.pallas import tpu as pltpu
from jax.sharding import PartitionSpec as P

ITERS = 3


coupling = 0.4


def exchange(block, axis, distance):
    count = lax.axis_size(axis)
    route = [(i, i ^ (1 << distance)) for i in range(count)]
    return lax.ppermute(block, axis, route)


def shifted(value, axis, step):
    count = lax.axis_size(axis)
    return lax.ppermute(value, axis, [(i, (i + step) % count) for i in range(count)])


def pair_product(own, partner, factor):
    both = jnp.concatenate([own, partner], axis=-1)
    weights = factor.reshape(2 * factor.shape[-2], factor.shape[-1])
    return jnp.dot(both, weights, preferred_element_type=jnp.float32)


def call(kernel, out_shape, operands, flops, scratch=()):
    in_specs = [
        pl.BlockSpec(memory_space=pltpu.SMEM if op.dtype == jnp.int32 else pltpu.VMEM)
        for op in operands
    ]
    size = sum(op.size * op.dtype.itemsize for op in operands)
    return pl.pallas_call(
        kernel,
        out_shape=out_shape,
        in_specs=in_specs,
        scratch_shapes=scratch,
        out_specs=jax.tree.map(lambda _: pl.BlockSpec(memory_space=pltpu.VMEM), out_shape),
        cost_estimate=pl.CostEstimate(flops=flops, bytes_accessed=size, transcendentals=0),
        compiler_params=pltpu.CompilerParams(vmem_limit_bytes=24 * 2**20),
    )(*operands)


def split_kernel(start, rows_ref, out_ref):
    blocks, _, width = out_ref.shape
    for b in range(blocks):
        out_ref[b] = rows_ref[:, (start + b) * width:(start + b + 1) * width]


def local_kernel(levels, z_ref, *refs):
    factors, out_ref = refs[:levels], refs[levels]
    blocks = z_ref.shape[0]
    mixed = [z_ref[b] for b in range(blocks)]
    for level, factor in enumerate(factors):
        stride = 1 << level
        mixed = [
            pair_product(mixed[b], mixed[b ^ stride], factor[b]).astype(jnp.bfloat16)
            for b in range(blocks)
        ]
    for b in range(blocks):
        out_ref[b] = mixed[b]


def level_kernel(own_ref, partner_ref, factor_ref, out_ref):
    for b in range(own_ref.shape[0]):
        out_ref[b] = pair_product(own_ref[b], partner_ref[b], factor_ref[b]).astype(jnp.bfloat16)


def near_kernel(start, index_ref, count_ref, *refs):
    pieces, near_ref, out_ref, window = refs[:-3], refs[-3], refs[-2], refs[-1]
    blocks, slots, width, _ = near_ref.shape
    half = pieces[0].shape[0]
    for i, piece in enumerate(pieces):
        window[i * half:(i + 1) * half] = piece[...]
    unused = len(pieces) * half
    window[unused] = jnp.zeros(window.shape[1:], window.dtype)
    for b in range(blocks):
        count = count_ref[start + b]
        taken = [
            window[jnp.where(k < count, index_ref[start + b, k], unused)] for k in range(slots)
        ]
        out_ref[b] = jnp.dot(
            jnp.concatenate(taken, axis=-1),
            near_ref[b].reshape(slots * width, width),
            preferred_element_type=jnp.float32,
        )


def last_kernel(own_ref, partner_ref, factor_ref, near_ref, source_ref, out_ref):
    for b in range(own_ref.shape[0]):
        mixed = pair_product(own_ref[b], partner_ref[b], factor_ref[b])
        mixed = mixed.astype(jnp.bfloat16).astype(jnp.float32)
        total = source_ref[b].astype(jnp.float32) - coupling * (mixed + near_ref[b])
        out_ref[b] = total.astype(jnp.bfloat16)


def join_kernel(*refs):
    parts, out_ref = refs[:-1], refs[-1]
    at = 0
    for part in parts:
        for b in range(part.shape[0]):
            width = part.shape[-1]
            out_ref[:, at:at + width] = part[b]
            at += width


def per_device(right_side, level_pairs, near_blocks, near_index, near_count):
    rhs_count = right_side.shape[0]
    blocks, slots, width, _ = near_blocks.shape
    levels = level_pairs.shape[0]
    level_bits = lax.axis_size("level").bit_length() - 1
    patch_bits = lax.axis_size("patch").bit_length() - 1
    local_levels = levels - level_bits - patch_bits
    half = 1 << local_levels
    chains = blocks // half
    piece = jax.ShapeDtypeStruct((half, rhs_count, width), jnp.bfloat16)
    near_shape = jax.ShapeDtypeStruct((half, rhs_count, width), jnp.float32)
    level_flops = 4 * half * rhs_count * width * width
    remote = [("level", i) for i in range(level_bits)] + [("patch", i) for i in range(patch_bits)]

    def factor(level, chain):
        return level_pairs[level, chain * half:(chain + 1) * half]

    near_parts = [near_blocks[c * half:(c + 1) * half] for c in range(chains)]
    source = [
        call(functools.partial(split_kernel, c * half), piece, (right_side,), 0)
        for c in range(chains)
    ]
    current = source
    window_shape = pltpu.VMEM((3 * blocks + 1, rhs_count, width), jnp.bfloat16)
    for sweep in range(ITERS):
        below = [shifted(current[c], "patch", 1) for c in range(chains)]
        above = [shifted(current[c], "patch", -1) for c in range(chains)]
        mixed = [
            call(
                functools.partial(local_kernel, local_levels),
                piece,
                (current[c], *[factor(i, c) for i in range(local_levels)]),
                local_levels * level_flops,
            )
            for c in range(chains)
        ]
        near = [
            call(
                functools.partial(near_kernel, c * half),
                near_shape,
                (near_index, near_count, *below, *current, *above, near_parts[c]),
                2 * half * slots * rhs_count * width * width,
                (window_shape,),
            )
            for c in range(chains)
        ]
        for i, (axis, bit) in enumerate(remote):
            partner = [exchange(mixed[c], axis, bit) for c in range(chains)]
            for c in range(chains):
                operands = (mixed[c], partner[c], factor(local_levels + i, c))
                if i < len(remote) - 1:
                    mixed[c] = call(level_kernel, piece, operands, level_flops)
                else:
                    mixed[c] = call(
                        last_kernel, piece, (*operands, near[c], source[c]), level_flops
                    )
        current = mixed
    return call(
        join_kernel,
        jax.ShapeDtypeStruct((rhs_count, blocks * width), jnp.bfloat16),
        current,
        0,
    )


def solution(mesh):
    in_specs = (
        P(None, ("patch", "level")),
        P(None, ("patch", "level"), None, None, None),
        P(("patch", "level"), None, None, None),
        P(("patch", "level"), None),
        P(("patch", "level")),
    )
    out_specs = P(None, ("patch", "level"))
    return jax.shard_map(
        per_device, mesh=mesh, in_specs=in_specs, out_specs=out_specs, check_vma=False
    )
```

```python
import functools

import jax
import jax.numpy as jnp
from jax import lax
from jax.experimental import pallas as pl
from jax.experimental.pallas import tpu as pltpu
from jax.sharding import PartitionSpec as P

ITERS = 3
CHAINS = 2
NEAR_RING = 1


coupling = 0.4


def exchange(block, axis, flip):
    route = [(i, i ^ flip) for i in range(lax.axis_size(axis))]
    return lax.ppermute(block, axis, route)


def shifted(value, axis, step):
    count = lax.axis_size(axis)
    return lax.ppermute(value, axis, [(i, (i + step) % count) for i in range(count)])


def pair_product(own, partner, factor):
    both = jnp.concatenate([own, partner], axis=-1)
    weights = factor.reshape(2 * factor.shape[-2], factor.shape[-1])
    return jnp.dot(both, weights, preferred_element_type=jnp.float32)


def place(array):
    return pl.BlockSpec(memory_space=pltpu.SMEM if array.dtype == jnp.int32 else pltpu.VMEM)


def call(kernel, out_shape, operands, flops, scratch=()):
    size = sum(op.size * op.dtype.itemsize for op in operands)
    return pl.pallas_call(
        kernel,
        out_shape=out_shape,
        in_specs=[place(op) for op in operands],
        scratch_shapes=scratch,
        out_specs=jax.tree.map(place, out_shape),
        cost_estimate=pl.CostEstimate(flops=flops, bytes_accessed=size, transcendentals=0),
        compiler_params=pltpu.CompilerParams(vmem_limit_bytes=8 * 2**20),
    )(*operands)


def split_kernel(start, rows_ref, out_ref):
    blocks, _, width = out_ref.shape
    for b in range(blocks):
        out_ref[b] = rows_ref[:, (start + b) * width:(start + b + 1) * width]


def local_kernel(start, z_ref, *refs):
    factors, out_ref = refs[:-1], refs[-1]
    blocks = z_ref.shape[0]
    mixed = [z_ref[b] for b in range(blocks)]
    for level, factor in enumerate(factors):
        mixed = [
            pair_product(mixed[b], mixed[b ^ (1 << level)], factor[0, start + b]).astype(
                jnp.bfloat16
            )
            for b in range(blocks)
        ]
    for b in range(blocks):
        out_ref[b] = mixed[b]


def level_kernel(start, own_ref, partner_ref, factor_ref, *refs):
    out_ref = refs[-1]
    for b in range(own_ref.shape[0]):
        out_ref[b] = pair_product(own_ref[b], partner_ref[b], factor_ref[0, start + b]).astype(
            jnp.bfloat16
        )


def near_kernel(start, index_ref, count_ref, *refs):
    pieces, near_ref, out_ref, window = refs[:-3], *refs[-3:]
    blocks = out_ref.shape[0]
    slots, width = near_ref.shape[1:3]
    unused = 0
    for piece in pieces:
        window[unused:unused + piece.shape[0]] = piece[...]
        unused += piece.shape[0]
    window[unused] = jnp.zeros(window.shape[1:], window.dtype)
    for b in range(start, start + blocks):
        count = count_ref[b]
        taken = [window[jnp.where(k < count, index_ref[k, b], unused)] for k in range(slots)]
        out_ref[b - start] = jnp.dot(
            jnp.concatenate(taken, axis=-1),
            near_ref[b].reshape(slots * width, width),
            preferred_element_type=jnp.float32,
        )


def take_kernel(*refs):
    refs[-1][...] = refs[-2][...]


def last_kernel(start, own_ref, partner_ref, factor_ref, near_ref, source_ref, out_ref):
    for b in range(own_ref.shape[0]):
        mixed = pair_product(own_ref[b], partner_ref[b], factor_ref[0, start + b])
        mixed = mixed.astype(jnp.bfloat16).astype(jnp.float32)
        total = source_ref[b].astype(jnp.float32) - coupling * (mixed + near_ref[b])
        out_ref[b] = total.astype(jnp.bfloat16)


def stack_kernel(*refs):
    at = 0
    for part in refs[:-1]:
        refs[-1][at:at + part.shape[0]] = part[...]
        at += part.shape[0]


def join_kernel(*refs):
    at = 0
    for part in refs[:-1]:
        for b in range(part.shape[0]):
            width = part.shape[-1]
            refs[-1][:, at:at + width] = part[b]
            at += width


def per_device(right_side, level_pairs, near_blocks, near_index, near_count):
    rhs_count = right_side.shape[0]
    blocks, slots, width, _ = near_blocks.shape
    levels = level_pairs.shape[0]
    level_bits = lax.axis_size("level").bit_length() - 1
    patch_bits = lax.axis_size("patch").bit_length() - 1
    core = levels - level_bits - patch_bits
    half = blocks // CHAINS
    chains = range(CHAINS)
    piece = jax.ShapeDtypeStruct((half, rhs_count, width), jnp.bfloat16)
    whole = jax.ShapeDtypeStruct((blocks, rhs_count, width), jnp.bfloat16)
    near_shape = jax.ShapeDtypeStruct((half, rhs_count, width), jnp.float32)
    one_level = jax.ShapeDtypeStruct((1, *level_pairs.shape[1:]), jnp.bfloat16)
    level_flops = 4 * half * rhs_count * width * width
    window_shape = pltpu.VMEM((3 * blocks + 1, rhs_count, width), jnp.bfloat16)

    rings = [
        (core + 1 + i, "level", 1 << (1 + i)) for i in range(0, level_bits - 1, 2)
    ] + [(core + level_bits + i, "patch", 1 << i) for i in range(0, patch_bits, 2)]
    factors = [level_pairs[level:level + 1] for level in range(levels)]
    partner_factors = {
        level: exchange(factors[level], axis, flip) for level, axis, flip in rings[1:]
    }

    def product(kernel, c, own, partner, factor, *more, shape=piece):
        return call(
            functools.partial(kernel, c * half), shape, (own, partner, factor, *more), level_flops
        )

    source = [
        call(functools.partial(split_kernel, c * half), piece, (right_side,), 0) for c in chains
    ]
    current = list(source)
    for sweep in range(ITERS):
        joined = call(stack_kernel, whole, current, 0)
        below = shifted(joined, "patch", 1)
        above = shifted(joined, "patch", -1)
        mixed = [
            call(
                functools.partial(local_kernel, c * half),
                piece,
                (current[c], *factors[:core]),
                core * level_flops,
            )
            for c in chains
        ]
        near = [
            call(
                functools.partial(near_kernel, c * half),
                near_shape,
                (near_index.T, near_count, below, joined, above, near_blocks),
                2 * half * slots * rhs_count * width * width,
                (window_shape,),
            )
            for c in chains
        ]
        for c in chains:
            partner = exchange(mixed[c], "level", 1)
            mixed[c] = product(level_kernel, c, mixed[c], partner, factors[core])
        for ring, (level, axis, flip) in enumerate(rings):
            for c in chains:
                partner = exchange(mixed[c], axis, flip)
                own = product(level_kernel, c, mixed[c], partner, factors[level])
                extra = (near[c],) if ring == NEAR_RING and sweep > 0 else ()
                if level in partner_factors:
                    theirs = product(
                        level_kernel, c, partner, mixed[c], partner_factors[level], *extra
                    )
                    partner = exchange(theirs, axis, 3 * flip)
                else:
                    partner = exchange(own, axis, 2 * flip)
                second = factors[level + 1]
                if ring == len(rings) - 1:
                    mixed[c] = product(last_kernel, c, own, partner, second, near[c], source[c])
                else:
                    mixed[c] = product(level_kernel, c, own, partner, second)
            if level not in partner_factors:
                partner_factors[level] = exchange(
                    call(take_kernel, one_level, (*mixed, factors[level]), 0), axis, flip
                )
        current = mixed
    return call(
        join_kernel,
        jax.ShapeDtypeStruct((rhs_count, blocks * width), jnp.bfloat16),
        current,
        0,
    )


def solution(mesh):
    in_specs = (
        P(None, ("patch", "level")),
        P(None, ("patch", "level"), None, None, None),
        P(("patch", "level"), None, None, None),
        P(("patch", "level"), None),
        P(("patch", "level")),
    )
    out_specs = P(None, ("patch", "level"))
    return jax.shard_map(
        per_device, mesh=mesh, in_specs=in_specs, out_specs=out_specs, check_vma=False
    )
```

```python
import functools

import jax
import jax.numpy as jnp
from jax import lax
from jax.experimental import pallas as pl
from jax.experimental.pallas import tpu as pltpu
from jax.sharding import PartitionSpec as P

ITERS = 3
CHAINS = 2
NEAR_TIES = ((1, 0, 0), (2, 0, 0))


coupling = 0.4


def exchange(block, axis, flip):
    route = [(i, i ^ flip) for i in range(lax.axis_size(axis))]
    return lax.ppermute(block, axis, route)


def shifted(value, axis, step):
    count = lax.axis_size(axis)
    return lax.ppermute(value, axis, [(i, (i + step) % count) for i in range(count)])


def pair_product(own, partner, factor):
    both = jnp.concatenate([own, partner], axis=-1)
    weights = factor.reshape(2 * factor.shape[-2], factor.shape[-1])
    return jnp.dot(both, weights, preferred_element_type=jnp.float32)


def place(array):
    return pl.BlockSpec(memory_space=pltpu.SMEM if array.dtype == jnp.int32 else pltpu.VMEM)


def call(kernel, out_shape, operands, flops, scratch=()):
    size = sum(op.size * op.dtype.itemsize for op in operands)
    return pl.pallas_call(
        kernel,
        out_shape=out_shape,
        in_specs=[place(op) for op in operands],
        scratch_shapes=scratch,
        out_specs=jax.tree.map(place, out_shape),
        cost_estimate=pl.CostEstimate(flops=flops, bytes_accessed=size, transcendentals=0),
        compiler_params=pltpu.CompilerParams(vmem_limit_bytes=8 * 2**20),
    )(*operands)


def split_kernel(start, rows_ref, out_ref):
    blocks, _, width = out_ref.shape
    for b in range(blocks):
        out_ref[b] = rows_ref[:, (start + b) * width:(start + b + 1) * width]


def local_kernel(levels, start, z_ref, factor_ref, out_ref):
    blocks = z_ref.shape[0]
    mixed = [z_ref[b] for b in range(blocks)]
    for level in range(levels):
        mixed = [
            pair_product(
                mixed[b], mixed[b ^ (1 << level)], factor_ref[level, start + b]
            ).astype(jnp.bfloat16)
            for b in range(blocks)
        ]
    for b in range(blocks):
        out_ref[b] = mixed[b]


def level_kernel(level, start, own_ref, partner_ref, factor_ref, *refs):
    out_ref = refs[-1]
    for b in range(own_ref.shape[0]):
        out_ref[b] = pair_product(own_ref[b], partner_ref[b], factor_ref[level, start + b]).astype(
            jnp.bfloat16
        )


def near_kernel(start, index_ref, count_ref, *refs):
    pieces, near_ref, out_ref, window = refs[:-3], *refs[-3:]
    blocks = out_ref.shape[0]
    slots, width = near_ref.shape[1:3]
    unused = 0
    for piece in pieces:
        window[unused:unused + piece.shape[0]] = piece[...]
        unused += piece.shape[0]
    window[unused] = jnp.zeros(window.shape[1:], window.dtype)
    for b in range(start, start + blocks):
        count = count_ref[b]
        taken = [window[jnp.where(k < count, index_ref[k, b], unused)] for k in range(slots)]
        out_ref[b - start] = jnp.dot(
            jnp.concatenate(taken, axis=-1),
            near_ref[b].reshape(slots * width, width),
            preferred_element_type=jnp.float32,
        )


def take_kernel(level, *refs):
    refs[-1][0] = refs[-2][level]


def last_kernel(level, start, own_ref, partner_ref, factor_ref, near_ref, source_ref, out_ref):
    for b in range(own_ref.shape[0]):
        mixed = pair_product(own_ref[b], partner_ref[b], factor_ref[level, start + b])
        mixed = mixed.astype(jnp.bfloat16).astype(jnp.float32)
        total = source_ref[b].astype(jnp.float32) - coupling * (mixed + near_ref[b])
        out_ref[b] = total.astype(jnp.bfloat16)


def stack_kernel(count, *refs):
    at = 0
    for part in refs[:count]:
        refs[-1][at:at + part.shape[0]] = part[...]
        at += part.shape[0]


def final_kernel(
    level, start, own_ref, partner_ref, factor_ref, near_ref, source_ref, before_ref, out_ref
):
    width = own_ref.shape[-1]
    for b in range(start):
        out_ref[:, b * width:(b + 1) * width] = before_ref[b]
    for b in range(own_ref.shape[0]):
        mixed = pair_product(own_ref[b], partner_ref[b], factor_ref[level, start + b])
        mixed = mixed.astype(jnp.bfloat16).astype(jnp.float32)
        total = source_ref[b].astype(jnp.float32) - coupling * (mixed + near_ref[b])
        at = (start + b) * width
        out_ref[:, at:at + width] = total.astype(jnp.bfloat16)


def per_device(right_side, level_pairs, near_blocks, near_index, near_count):
    rhs_count = right_side.shape[0]
    blocks, slots, width, _ = near_blocks.shape
    levels = level_pairs.shape[0]
    level_bits = lax.axis_size("level").bit_length() - 1
    patch_bits = lax.axis_size("patch").bit_length() - 1
    core = levels - level_bits - patch_bits
    half = blocks // CHAINS
    chains = range(CHAINS)
    piece = jax.ShapeDtypeStruct((half, rhs_count, width), jnp.bfloat16)
    whole = jax.ShapeDtypeStruct((blocks, rhs_count, width), jnp.bfloat16)
    near_shape = jax.ShapeDtypeStruct((half, rhs_count, width), jnp.float32)
    one_level = jax.ShapeDtypeStruct((1, *level_pairs.shape[1:]), jnp.bfloat16)
    flat = jax.ShapeDtypeStruct(right_side.shape, jnp.bfloat16)
    level_flops = 4 * half * rhs_count * width * width
    window_shape = pltpu.VMEM((3 * blocks + 1, rhs_count, width), jnp.bfloat16)

    rings = [
        (core + 1 + i, "level", 1 << (1 + i)) for i in range(0, level_bits - 1, 2)
    ] + [(core + level_bits + i, "patch", 1 << i) for i in range(0, patch_bits, 2)]
    early = level_pairs[:core + 1]
    factors = [(early, level) for level in range(core + 1)]
    factors += [(level_pairs, level) for level in range(core + 1, levels)]

    def sent(level, axis, flip, after):
        taken = call(functools.partial(take_kernel, level), one_level, (*after, level_pairs), 0)
        return exchange(taken, axis, flip)

    level, axis, flip = rings[1]
    partner_factors = {level: exchange(level_pairs[level:level + 1], axis, flip)}

    def product(kernel, c, own, partner, factor, *more, shape=piece):
        pairs, level = factor
        return call(
            functools.partial(kernel, level, c * half),
            shape,
            (own, partner, pairs, *more),
            level_flops,
        )

    source = [
        call(functools.partial(split_kernel, c * half), piece, (right_side,), 0) for c in chains
    ]
    current = list(source)
    for sweep in range(ITERS):
        mixed = [
            call(
                functools.partial(local_kernel, core, c * half),
                piece,
                (current[c], early),
                core * level_flops,
            )
            for c in chains
        ]
        def window_of(*after):
            joined = call(functools.partial(stack_kernel, CHAINS), whole, (*current, *after), 0)
            return shifted(joined, "patch", 1), joined, shifted(joined, "patch", -1)

        def near_of(c):
            return call(
                functools.partial(near_kernel, c * half),
                near_shape,
                (near_index.T, near_count, *window, near_blocks),
                2 * half * slots * rhs_count * width * width,
                (window_shape,),
            )

        ties = {(2, 0, 0): near_blocks}
        if sweep > 0:
            ties = {}
            window = window_of()
            near = [near_of(c) for c in chains]
            ties[0, 1, 0] = window[0]
            for c in chains:
                ties[NEAR_TIES[c]] = near[c]
        for c in chains:
            partner = exchange(mixed[c], "level", 1)
            mixed[c] = product(level_kernel, c, mixed[c], partner, factors[core])
        if sweep == 0:
            for level, axis, flip in rings[2:]:
                partner_factors[level] = sent(level, axis, flip, mixed)
        for ring, (level, axis, flip) in enumerate(rings):
            for c in chains:
                partner = exchange(mixed[c], axis, flip)
                own = product(level_kernel, c, mixed[c], partner, factors[level])
                extra = [ties[ring, 0, c]] if (ring, 0, c) in ties else []
                more = [ties[ring, 1, c]] if (ring, 1, c) in ties else []
                if level in partner_factors:
                    theirs = product(
                        level_kernel, c, partner, mixed[c], (partner_factors[level], 0), *extra
                    )
                    partner = exchange(theirs, axis, 3 * flip)
                else:
                    partner = exchange(own, axis, 2 * flip)
                second = factors[level + 1]
                if ring == len(rings) - 1 and sweep == ITERS - 1 and c == CHAINS - 1:
                    mixed[c] = product(
                        final_kernel, c, own, partner, second, near[c], source[c], mixed[0],
                        shape=flat,
                    )
                elif ring == len(rings) - 1:
                    mixed[c] = product(last_kernel, c, own, partner, second, near[c], source[c])
                else:
                    mixed[c] = product(level_kernel, c, own, partner, second, *more)
            if sweep == 0 and ring == 1:
                window = window_of(mixed[0])
                near = [near_of(c) for c in chains]
            if level not in partner_factors:
                partner_factors[level] = sent(level, axis, flip, mixed)
        current = mixed
    return current[-1]


def solution(mesh):
    in_specs = (
        P(None, ("patch", "level")),
        P(None, ("patch", "level"), None, None, None),
        P(("patch", "level"), None, None, None),
        P(("patch", "level"), None),
        P(("patch", "level")),
    )
    out_specs = P(None, ("patch", "level"))
    return jax.shard_map(
        per_device, mesh=mesh, in_specs=in_specs, out_specs=out_specs, check_vma=False
    )
```

```python
import functools

import jax
import jax.numpy as jnp
from jax import lax
from jax.experimental import pallas as pl
from jax.experimental.pallas import tpu as pltpu
from jax.sharding import PartitionSpec as P

ITERS = 3
CHAINS = 2
NEAR_TIES = ((1, 0, 0), (2, 0, 0))


coupling = 0.4


def exchange(block, axis, flip):
    route = [(i, i ^ flip) for i in range(lax.axis_size(axis))]
    return lax.ppermute(block, axis, route)


def exchange_next(block, axis):
    count = lax.axis_size(axis)
    route = []
    for i in range(1, count, 2):
        route += [(i, (i + 1) % count), ((i + 1) % count, i)]
    return lax.ppermute(block, axis, route)


def pair_product(own, partner, factor):
    both = jnp.concatenate([own, partner], axis=-1)
    weights = factor.reshape(2 * factor.shape[-2], factor.shape[-1])
    return jnp.dot(both, weights, preferred_element_type=jnp.float32)


def place(array):
    return pl.BlockSpec(memory_space=pltpu.SMEM if array.dtype == jnp.int32 else pltpu.VMEM)


def call(kernel, out_shape, operands, flops, scratch=()):
    size = sum(op.size * op.dtype.itemsize for op in operands)
    return pl.pallas_call(
        kernel,
        out_shape=out_shape,
        in_specs=[place(op) for op in operands],
        scratch_shapes=scratch,
        out_specs=jax.tree.map(place, out_shape),
        cost_estimate=pl.CostEstimate(flops=flops, bytes_accessed=size, transcendentals=0),
        compiler_params=pltpu.CompilerParams(vmem_limit_bytes=8 * 2**20),
    )(*operands)


def split_kernel(start, rows_ref, out_ref):
    blocks, _, width = out_ref.shape
    for b in range(blocks):
        out_ref[b] = rows_ref[:, (start + b) * width:(start + b + 1) * width]


def local_kernel(levels, start, z_ref, factor_ref, out_ref):
    blocks = z_ref.shape[0]
    mixed = [z_ref[b] for b in range(blocks)]
    for level in range(levels):
        mixed = [
            pair_product(
                mixed[b], mixed[b ^ (1 << level)], factor_ref[level, start + b]
            ).astype(jnp.bfloat16)
            for b in range(blocks)
        ]
    for b in range(blocks):
        out_ref[b] = mixed[b]


def level_kernel(level, start, own_ref, partner_ref, factor_ref, *refs):
    out_ref = refs[-1]
    for b in range(own_ref.shape[0]):
        out_ref[b] = pair_product(own_ref[b], partner_ref[b], factor_ref[level, start + b]).astype(
            jnp.bfloat16
        )


def near_kernel(start, index_ref, count_ref, *refs):
    pieces, near_ref, out_ref, window = refs[:-3], *refs[-3:]
    blocks = out_ref.shape[0]
    slots, width = near_ref.shape[1:3]
    unused = 0
    for piece in pieces:
        window[unused:unused + piece.shape[0]] = piece[...]
        unused += piece.shape[0]
    window[unused] = jnp.zeros(window.shape[1:], window.dtype)
    last = 2 * near_ref.shape[0]
    even = lax.axis_index("patch") % 2 == 0
    below, above = jnp.where(even, last, 0), jnp.where(even, -last, 0)

    def place_of(k, b):
        at = index_ref[k, b]
        shift = jnp.where(at < last // 2, below, jnp.where(at < last, 0, above))
        return jnp.where(k < count_ref[b], at + shift, unused)

    for b in range(start, start + blocks):
        taken = [window[place_of(k, b)] for k in range(slots)]
        out_ref[b - start] = jnp.dot(
            jnp.concatenate(taken, axis=-1),
            near_ref[b].reshape(slots * width, width),
            preferred_element_type=jnp.float32,
        )


def take_kernel(level, *refs):
    refs[-1][0] = refs[-2][level]


def last_kernel(level, start, own_ref, partner_ref, factor_ref, near_ref, source_ref, out_ref):
    for b in range(own_ref.shape[0]):
        mixed = pair_product(own_ref[b], partner_ref[b], factor_ref[level, start + b])
        mixed = mixed.astype(jnp.bfloat16).astype(jnp.float32)
        total = source_ref[b].astype(jnp.float32) - coupling * (mixed + near_ref[b])
        out_ref[b] = total.astype(jnp.bfloat16)


def stack_kernel(count, *refs):
    at = 0
    for part in refs[:count]:
        refs[-1][at:at + part.shape[0]] = part[...]
        at += part.shape[0]


def final_kernel(
    level, start, own_ref, partner_ref, factor_ref, near_ref, source_ref, before_ref, out_ref
):
    width = own_ref.shape[-1]
    for b in range(start):
        out_ref[:, b * width:(b + 1) * width] = before_ref[b]
    for b in range(own_ref.shape[0]):
        mixed = pair_product(own_ref[b], partner_ref[b], factor_ref[level, start + b])
        mixed = mixed.astype(jnp.bfloat16).astype(jnp.float32)
        total = source_ref[b].astype(jnp.float32) - coupling * (mixed + near_ref[b])
        at = (start + b) * width
        out_ref[:, at:at + width] = total.astype(jnp.bfloat16)


def per_device(right_side, level_pairs, near_blocks, near_index, near_count):
    rhs_count = right_side.shape[0]
    blocks, slots, width, _ = near_blocks.shape
    levels = level_pairs.shape[0]
    level_bits = lax.axis_size("level").bit_length() - 1
    patch_bits = lax.axis_size("patch").bit_length() - 1
    core = levels - level_bits - patch_bits
    half = blocks // CHAINS
    chains = range(CHAINS)
    piece = jax.ShapeDtypeStruct((half, rhs_count, width), jnp.bfloat16)
    whole = jax.ShapeDtypeStruct((blocks, rhs_count, width), jnp.bfloat16)
    near_shape = jax.ShapeDtypeStruct((half, rhs_count, width), jnp.float32)
    one_level = jax.ShapeDtypeStruct((1, *level_pairs.shape[1:]), jnp.bfloat16)
    flat = jax.ShapeDtypeStruct(right_side.shape, jnp.bfloat16)
    level_flops = 4 * half * rhs_count * width * width
    window_shape = pltpu.VMEM((3 * blocks + 1, rhs_count, width), jnp.bfloat16)

    rings = [
        (core + 1 + i, "level", 1 << (1 + i)) for i in range(0, level_bits - 1, 2)
    ] + [(core + level_bits + i, "patch", 1 << i) for i in range(0, patch_bits, 2)]
    early = level_pairs[:core + 1]
    factors = [(early, level) for level in range(core + 1)]
    factors += [(level_pairs, level) for level in range(core + 1, levels)]

    def sent(level, axis, flip, after):
        taken = call(functools.partial(take_kernel, level), one_level, (*after, level_pairs), 0)
        return exchange(taken, axis, flip)

    partner_factors = {
        level: exchange(level_pairs[level:level + 1], axis, flip) for level, axis, flip in rings[1:]
    }

    def product(kernel, c, own, partner, factor, *more, shape=piece):
        pairs, level = factor
        return call(
            functools.partial(kernel, level, c * half),
            shape,
            (own, partner, pairs, *more),
            level_flops,
        )

    source = [
        call(functools.partial(split_kernel, c * half), piece, (right_side,), 0) for c in chains
    ]
    current = list(source)
    for sweep in range(ITERS):
        mixed = [
            call(
                functools.partial(local_kernel, core, c * half),
                piece,
                (current[c], early),
                core * level_flops,
            )
            for c in chains
        ]
        def window_of(*after):
            joined = call(functools.partial(stack_kernel, CHAINS), whole, (*current, *after), 0)
            return exchange(joined, "patch", 1), joined, exchange_next(joined, "patch")

        def near_of(c):
            return call(
                functools.partial(near_kernel, c * half),
                near_shape,
                (near_index.T, near_count, *window, near_blocks),
                2 * half * slots * rhs_count * width * width,
                (window_shape,),
            )

        ties = {(2, 0, 0): near_blocks}
        if sweep > 0:
            ties = {}
            window = window_of()
            near = [near_of(c) for c in chains]
            ties[0, 1, 0] = window[0]
            for c in chains:
                ties[NEAR_TIES[c]] = near[c]
        for c in chains:
            partner = exchange(mixed[c], "level", 1)
            mixed[c] = product(level_kernel, c, mixed[c], partner, factors[core])
        for ring, (level, axis, flip) in enumerate(rings):
            for c in chains:
                partner = exchange(mixed[c], axis, flip)
                own = product(level_kernel, c, mixed[c], partner, factors[level])
                extra = [ties[ring, 0, c]] if (ring, 0, c) in ties else []
                more = [ties[ring, 1, c]] if (ring, 1, c) in ties else []
                if level in partner_factors:
                    theirs = product(
                        level_kernel, c, partner, mixed[c], (partner_factors[level], 0), *extra
                    )
                    partner = exchange(theirs, axis, 3 * flip)
                else:
                    partner = exchange(own, axis, 2 * flip)
                second = factors[level + 1]
                if ring == len(rings) - 1 and sweep == ITERS - 1 and c == CHAINS - 1:
                    mixed[c] = product(
                        final_kernel, c, own, partner, second, near[c], source[c], mixed[0],
                        shape=flat,
                    )
                elif ring == len(rings) - 1:
                    mixed[c] = product(last_kernel, c, own, partner, second, near[c], source[c])
                else:
                    mixed[c] = product(level_kernel, c, own, partner, second, *more)
            if sweep == 0 and ring == 1:
                window = window_of(mixed[0])
                near = [near_of(c) for c in chains]
            if level not in partner_factors:
                partner_factors[level] = sent(level, axis, flip, mixed)
        current = mixed
    return current[-1]


def solution(mesh):
    in_specs = (
        P(None, ("patch", "level")),
        P(None, ("patch", "level"), None, None, None),
        P(("patch", "level"), None, None, None),
        P(("patch", "level"), None),
        P(("patch", "level")),
    )
    out_specs = P(None, ("patch", "level"))
    return jax.shard_map(
        per_device, mesh=mesh, in_specs=in_specs, out_specs=out_specs, check_vma=False
    )
```

```python
import functools

import jax
import jax.numpy as jnp
from jax import lax
from jax.experimental import pallas as pl
from jax.experimental.pallas import tpu as pltpu
from jax.sharding import PartitionSpec as P

ITERS = 3
CHAINS = 2
NEAR_TIES = ((1, 0, 0), (2, 0, 0))


coupling = 0.4


def exchange(block, axis, flip):
    route = [(i, i ^ flip) for i in range(lax.axis_size(axis))]
    return lax.ppermute(block, axis, route)


def exchange_next(block, axis):
    count = lax.axis_size(axis)
    route = []
    for i in range(1, count, 2):
        route += [(i, (i + 1) % count), ((i + 1) % count, i)]
    return lax.ppermute(block, axis, route)


def pair_product(own, partner, factor):
    both = jnp.concatenate([own, partner], axis=-1)
    weights = factor.reshape(2 * factor.shape[-2], factor.shape[-1])
    return jnp.dot(both, weights, preferred_element_type=jnp.float32)


def place(array):
    return pl.BlockSpec(memory_space=pltpu.SMEM if array.dtype == jnp.int32 else pltpu.VMEM)


def call(kernel, out_shape, operands, flops, scratch=()):
    size = sum(op.size * op.dtype.itemsize for op in operands)
    return pl.pallas_call(
        kernel,
        out_shape=out_shape,
        in_specs=[place(op) for op in operands],
        scratch_shapes=scratch,
        out_specs=jax.tree.map(place, out_shape),
        cost_estimate=pl.CostEstimate(flops=flops, bytes_accessed=size, transcendentals=0),
        compiler_params=pltpu.CompilerParams(vmem_limit_bytes=8 * 2**20),
    )(*operands)


def split_kernel(start, rows_ref, out_ref):
    blocks, _, width = out_ref.shape
    for b in range(blocks):
        out_ref[b] = rows_ref[:, (start + b) * width:(start + b + 1) * width]


def local_kernel(levels, start, z_ref, factor_ref, out_ref):
    blocks = z_ref.shape[0]
    mixed = [z_ref[b] for b in range(blocks)]
    for level in range(levels):
        mixed = [
            pair_product(
                mixed[b], mixed[b ^ (1 << level)], factor_ref[level, start + b]
            ).astype(jnp.bfloat16)
            for b in range(blocks)
        ]
    for b in range(blocks):
        out_ref[b] = mixed[b]


def level_kernel(level, start, own_ref, partner_ref, factor_ref, *refs):
    out_ref = refs[-1]
    for b in range(own_ref.shape[0]):
        out_ref[b] = pair_product(own_ref[b], partner_ref[b], factor_ref[level, start + b]).astype(
            jnp.bfloat16
        )


def near_kernel(start, index_ref, count_ref, *refs):
    pieces, near_ref, out_ref, window = refs[:-3], *refs[-3:]
    blocks = out_ref.shape[0]
    slots, width = near_ref.shape[1:3]
    unused = 0
    for piece in pieces:
        window[unused:unused + piece.shape[0]] = piece[...]
        unused += piece.shape[0]
    window[unused] = jnp.zeros(window.shape[1:], window.dtype)
    last = 2 * near_ref.shape[0]
    even = lax.axis_index("patch") % 2 == 0
    below, above = jnp.where(even, last, 0), jnp.where(even, -last, 0)

    def place_of(k, b):
        at = index_ref[k, b]
        shift = jnp.where(at < last // 2, below, jnp.where(at < last, 0, above))
        return jnp.where(k < count_ref[b], at + shift, unused)

    for b in range(start, start + blocks):
        taken = [window[place_of(k, b)] for k in range(slots)]
        out_ref[b - start] = jnp.dot(
            jnp.concatenate(taken, axis=-1),
            near_ref[b].reshape(slots * width, width),
            preferred_element_type=jnp.float32,
        )


def take_kernel(level, *refs):
    refs[-1][0] = refs[-2][level]


def last_kernel(level, start, own_ref, partner_ref, factor_ref, near_ref, source_ref, out_ref):
    for b in range(own_ref.shape[0]):
        mixed = pair_product(own_ref[b], partner_ref[b], factor_ref[level, start + b])
        mixed = mixed.astype(jnp.bfloat16).astype(jnp.float32)
        total = source_ref[b].astype(jnp.float32) - coupling * (mixed + near_ref[b])
        out_ref[b] = total.astype(jnp.bfloat16)


def stack_kernel(count, *refs):
    at = 0
    for part in refs[:count]:
        refs[-1][at:at + part.shape[0]] = part[...]
        at += part.shape[0]


def final_kernel(
    level, start, own_ref, partner_ref, factor_ref, near_ref, source_ref, before_ref, out_ref
):
    width = own_ref.shape[-1]
    for b in range(start):
        out_ref[:, b * width:(b + 1) * width] = before_ref[b]
    for b in range(own_ref.shape[0]):
        mixed = pair_product(own_ref[b], partner_ref[b], factor_ref[level, start + b])
        mixed = mixed.astype(jnp.bfloat16).astype(jnp.float32)
        total = source_ref[b].astype(jnp.float32) - coupling * (mixed + near_ref[b])
        at = (start + b) * width
        out_ref[:, at:at + width] = total.astype(jnp.bfloat16)


def per_device(right_side, level_pairs, near_blocks, near_index, near_count):
    rhs_count = right_side.shape[0]
    blocks, slots, width, _ = near_blocks.shape
    levels = level_pairs.shape[0]
    level_bits = lax.axis_size("level").bit_length() - 1
    patch_bits = lax.axis_size("patch").bit_length() - 1
    core = levels - level_bits - patch_bits
    half = blocks // CHAINS
    chains = range(CHAINS)
    piece = jax.ShapeDtypeStruct((half, rhs_count, width), jnp.bfloat16)
    whole = jax.ShapeDtypeStruct((blocks, rhs_count, width), jnp.bfloat16)
    near_shape = jax.ShapeDtypeStruct((half, rhs_count, width), jnp.float32)
    one_level = jax.ShapeDtypeStruct((1, *level_pairs.shape[1:]), jnp.bfloat16)
    flat = jax.ShapeDtypeStruct(right_side.shape, jnp.bfloat16)
    level_flops = 4 * half * rhs_count * width * width
    window_shape = pltpu.VMEM((3 * blocks + 1, rhs_count, width), jnp.bfloat16)

    rings = [
        (core + 1 + i, "level", 1 << (1 + i)) for i in range(0, level_bits - 1, 2)
    ] + [(core + level_bits + i, "patch", 1 << i) for i in range(0, patch_bits, 2)]
    early = level_pairs[:core + 1]
    factors = [(early, level) for level in range(core + 1)]
    factors += [(level_pairs, level) for level in range(core + 1, levels)]

    def sent(level, axis, flip, after):
        taken = call(functools.partial(take_kernel, level), one_level, (*after, level_pairs), 0)
        return exchange(taken, axis, flip)

    partner_factors = {
        level: exchange(level_pairs[level:level + 1], axis, flip) for level, axis, flip in rings[1:]
    }

    def product(kernel, c, own, partner, factor, *more, shape=piece):
        pairs, level = factor
        return call(
            functools.partial(kernel, level, c * half),
            shape,
            (own, partner, pairs, *more),
            level_flops,
        )

    source = [
        call(functools.partial(split_kernel, c * half), piece, (right_side,), 0) for c in chains
    ]
    current = list(source)
    for sweep in range(ITERS):
        mixed = [
            call(
                functools.partial(local_kernel, core, c * half),
                piece,
                (current[c], early),
                core * level_flops,
            )
            for c in chains
        ]
        def window_of(*after):
            joined = call(functools.partial(stack_kernel, CHAINS), whole, (*current, *after), 0)
            return exchange(joined, "patch", 1), joined, exchange_next(joined, "patch")

        def near_of(c):
            return call(
                functools.partial(near_kernel, c * half),
                near_shape,
                (near_index.T, near_count, *window, near_blocks),
                2 * half * slots * rhs_count * width * width,
                (window_shape,),
            )

        ties = {(2, 0, 0): near_blocks}
        if sweep > 0:
            ties = {}
            window = window_of()
            near = [near_of(c) for c in chains]
            ties[0, 1, 0] = window[2]
            for c in chains:
                ties[NEAR_TIES[c]] = near[c]
        for c in chains:
            partner = exchange(mixed[c], "level", 1)
            mixed[c] = product(level_kernel, c, mixed[c], partner, factors[core])
        for ring, (level, axis, flip) in enumerate(rings):
            for c in chains:
                partner = exchange(mixed[c], axis, flip)
                own = product(level_kernel, c, mixed[c], partner, factors[level])
                extra = [ties[ring, 0, c]] if (ring, 0, c) in ties else []
                more = [ties[ring, 1, c]] if (ring, 1, c) in ties else []
                if level in partner_factors:
                    theirs = product(
                        level_kernel, c, partner, mixed[c], (partner_factors[level], 0), *extra
                    )
                    partner = exchange(theirs, axis, 3 * flip)
                else:
                    partner = exchange(own, axis, 2 * flip)
                second = factors[level + 1]
                if ring == len(rings) - 1 and sweep == ITERS - 1 and c == CHAINS - 1:
                    mixed[c] = product(
                        final_kernel, c, own, partner, second, near[c], source[c], mixed[0],
                        shape=flat,
                    )
                elif ring == len(rings) - 1:
                    mixed[c] = product(last_kernel, c, own, partner, second, near[c], source[c])
                else:
                    mixed[c] = product(level_kernel, c, own, partner, second, *more)
            if sweep == 0 and ring == 1:
                window = window_of(mixed[0])
                near = [near_of(c) for c in chains]
            if level not in partner_factors:
                partner_factors[level] = sent(level, axis, flip, mixed)
        current = mixed
    return current[-1]


def solution(mesh):
    in_specs = (
        P(None, ("patch", "level")),
        P(None, ("patch", "level"), None, None, None),
        P(("patch", "level"), None, None, None),
        P(("patch", "level"), None),
        P(("patch", "level")),
    )
    out_specs = P(None, ("patch", "level"))
    return jax.shard_map(
        per_device, mesh=mesh, in_specs=in_specs, out_specs=out_specs, check_vma=False
    )
```

```python
import functools

import jax
import jax.numpy as jnp
from jax import lax
from jax.experimental import pallas as pl
from jax.experimental.pallas import tpu as pltpu
from jax.sharding import PartitionSpec as P

ITERS = 3
CHAINS = 2
NEAR_TIES = ((1, 0, 0), (2, 0, 0))


coupling = 0.4


def exchange(block, axis, flip):
    route = [(i, i ^ flip) for i in range(lax.axis_size(axis))]
    return lax.ppermute(block, axis, route)


def exchange_next(block, axis):
    count = lax.axis_size(axis)
    route = []
    for i in range(1, count, 2):
        route += [(i, (i + 1) % count), ((i + 1) % count, i)]
    return lax.ppermute(block, axis, route)


def pair_product(own, partner, factor):
    both = jnp.concatenate([own, partner], axis=-1)
    weights = factor.reshape(2 * factor.shape[-2], factor.shape[-1])
    return jnp.dot(both, weights, preferred_element_type=jnp.float32)


def place(array):
    return pl.BlockSpec(memory_space=pltpu.SMEM if array.dtype == jnp.int32 else pltpu.VMEM)


def call(kernel, out_shape, operands, flops, scratch=()):
    size = sum(op.size * op.dtype.itemsize for op in operands)
    return pl.pallas_call(
        kernel,
        out_shape=out_shape,
        in_specs=[place(op) for op in operands],
        scratch_shapes=scratch,
        out_specs=jax.tree.map(place, out_shape),
        cost_estimate=pl.CostEstimate(flops=flops, bytes_accessed=size, transcendentals=0),
        compiler_params=pltpu.CompilerParams(vmem_limit_bytes=8 * 2**20),
    )(*operands)


def split_kernel(start, rows_ref, out_ref):
    blocks, _, width = out_ref.shape
    for b in range(blocks):
        out_ref[b] = rows_ref[:, (start + b) * width:(start + b + 1) * width]


def local_kernel(levels, start, z_ref, factor_ref, out_ref):
    blocks = z_ref.shape[0]
    mixed = [z_ref[b] for b in range(blocks)]
    for level in range(levels):
        mixed = [
            pair_product(
                mixed[b], mixed[b ^ (1 << level)], factor_ref[level, start + b]
            ).astype(jnp.bfloat16)
            for b in range(blocks)
        ]
    for b in range(blocks):
        out_ref[b] = mixed[b]


def level_kernel(level, start, own_ref, partner_ref, factor_ref, *refs):
    out_ref = refs[-1]
    for b in range(own_ref.shape[0]):
        out_ref[b] = pair_product(own_ref[b], partner_ref[b], factor_ref[level, start + b]).astype(
            jnp.bfloat16
        )


def near_kernel(start, index_ref, count_ref, *refs):
    pieces, near_ref, out_ref, window = refs[:-3], *refs[-3:]
    blocks = out_ref.shape[0]
    slots, width = near_ref.shape[1:3]
    unused = 0
    for piece in pieces:
        window[unused:unused + piece.shape[0]] = piece[...]
        unused += piece.shape[0]
    window[unused] = jnp.zeros(window.shape[1:], window.dtype)
    last = 2 * near_ref.shape[0]
    even = lax.axis_index("patch") % 2 == 0
    below, above = jnp.where(even, last, 0), jnp.where(even, -last, 0)

    def place_of(k, b):
        at = index_ref[k, b]
        shift = jnp.where(at < last // 2, below, jnp.where(at < last, 0, above))
        return jnp.where(k < count_ref[b], at + shift, unused)

    for b in range(start, start + blocks):
        taken = [window[place_of(k, b)] for k in range(slots)]
        out_ref[b - start] = jnp.dot(
            jnp.concatenate(taken, axis=-1),
            near_ref[b].reshape(slots * width, width),
            preferred_element_type=jnp.float32,
        )


def take_kernel(level, *refs):
    refs[-1][0] = refs[-2][level]


def last_kernel(level, start, own_ref, partner_ref, factor_ref, near_ref, source_ref, out_ref):
    for b in range(own_ref.shape[0]):
        mixed = pair_product(own_ref[b], partner_ref[b], factor_ref[level, start + b])
        mixed = mixed.astype(jnp.bfloat16).astype(jnp.float32)
        total = source_ref[b].astype(jnp.float32) - coupling * (mixed + near_ref[b])
        out_ref[b] = total.astype(jnp.bfloat16)


def stack_kernel(count, *refs):
    at = 0
    for part in refs[:count]:
        refs[-1][at:at + part.shape[0]] = part[...]
        at += part.shape[0]


def final_kernel(
    level, start, own_ref, partner_ref, factor_ref, near_ref, source_ref, before_ref, out_ref
):
    width = own_ref.shape[-1]
    for b in range(start):
        out_ref[:, b * width:(b + 1) * width] = before_ref[b]
    for b in range(own_ref.shape[0]):
        mixed = pair_product(own_ref[b], partner_ref[b], factor_ref[level, start + b])
        mixed = mixed.astype(jnp.bfloat16).astype(jnp.float32)
        total = source_ref[b].astype(jnp.float32) - coupling * (mixed + near_ref[b])
        at = (start + b) * width
        out_ref[:, at:at + width] = total.astype(jnp.bfloat16)


def per_device(right_side, level_pairs, near_blocks, near_index, near_count):
    rhs_count = right_side.shape[0]
    blocks, slots, width, _ = near_blocks.shape
    levels = level_pairs.shape[0]
    level_bits = lax.axis_size("level").bit_length() - 1
    patch_bits = lax.axis_size("patch").bit_length() - 1
    core = levels - level_bits - patch_bits
    half = blocks // CHAINS
    chains = range(CHAINS)
    piece = jax.ShapeDtypeStruct((half, rhs_count, width), jnp.bfloat16)
    whole = jax.ShapeDtypeStruct((blocks, rhs_count, width), jnp.bfloat16)
    near_shape = jax.ShapeDtypeStruct((half, rhs_count, width), jnp.float32)
    one_level = jax.ShapeDtypeStruct((1, *level_pairs.shape[1:]), jnp.bfloat16)
    flat = jax.ShapeDtypeStruct(right_side.shape, jnp.bfloat16)
    level_flops = 4 * half * rhs_count * width * width
    window_shape = pltpu.VMEM((3 * blocks + 1, rhs_count, width), jnp.bfloat16)

    rings = [
        (core + 1 + i, "level", 1 << (1 + i)) for i in range(0, level_bits - 1, 2)
    ] + [(core + level_bits + i, "patch", 1 << i) for i in range(0, patch_bits, 2)]
    early = level_pairs[:core + 1]
    factors = [(early, level) for level in range(core + 1)]
    factors += [(level_pairs, level) for level in range(core + 1, levels)]

    def sent(level, axis, flip, after):
        taken = call(functools.partial(take_kernel, level), one_level, (*after, level_pairs), 0)
        return exchange(taken, axis, flip)

    partner_factors = {
        level: exchange(level_pairs[level:level + 1], axis, flip) for level, axis, flip in rings[1:]
    }

    def product(kernel, c, own, partner, factor, *more, shape=piece):
        pairs, level = factor
        return call(
            functools.partial(kernel, level, c * half),
            shape,
            (own, partner, pairs, *more),
            level_flops,
        )

    source = [
        call(functools.partial(split_kernel, c * half), piece, (right_side,), 0) for c in chains
    ]
    current = list(source)
    for sweep in range(ITERS):
        mixed = [
            call(
                functools.partial(local_kernel, core, c * half),
                piece,
                (current[c], early),
                core * level_flops,
            )
            for c in chains
        ]
        def window_of(*after):
            joined = call(functools.partial(stack_kernel, CHAINS), whole, (*current, *after), 0)
            return exchange(joined, "patch", 1), joined, exchange_next(joined, "patch")

        def near_of(c):
            return call(
                functools.partial(near_kernel, c * half),
                near_shape,
                (near_index.T, near_count, *window, near_blocks),
                2 * half * slots * rhs_count * width * width,
                (window_shape,),
            )

        ties = {(2, 0, 0): near_blocks}
        if sweep > 0:
            ties = {}
            window = window_of()
            near = [near_of(c) for c in chains]
            ties[0, 1, 0] = window[2]
            ties[0, 1, 1] = window[0]
            for c in chains:
                ties[NEAR_TIES[c]] = near[c]
        for c in chains:
            partner = exchange(mixed[c], "level", 1)
            mixed[c] = product(level_kernel, c, mixed[c], partner, factors[core])
        for ring, (level, axis, flip) in enumerate(rings):
            for c in chains:
                partner = exchange(mixed[c], axis, flip)
                own = product(level_kernel, c, mixed[c], partner, factors[level])
                extra = [ties[ring, 0, c]] if (ring, 0, c) in ties else []
                more = [ties[ring, 1, c]] if (ring, 1, c) in ties else []
                if level in partner_factors:
                    theirs = product(
                        level_kernel, c, partner, mixed[c], (partner_factors[level], 0), *extra
                    )
                    partner = exchange(theirs, axis, 3 * flip)
                else:
                    partner = exchange(own, axis, 2 * flip)
                second = factors[level + 1]
                if ring == len(rings) - 1 and sweep == ITERS - 1 and c == CHAINS - 1:
                    mixed[c] = product(
                        final_kernel, c, own, partner, second, near[c], source[c], mixed[0],
                        shape=flat,
                    )
                elif ring == len(rings) - 1:
                    mixed[c] = product(last_kernel, c, own, partner, second, near[c], source[c])
                else:
                    mixed[c] = product(level_kernel, c, own, partner, second, *more)
            if sweep == 0 and ring == 1:
                window = window_of(mixed[0])
                near = [near_of(c) for c in chains]
            if level not in partner_factors:
                partner_factors[level] = sent(level, axis, flip, mixed)
        current = mixed
    return current[-1]


def solution(mesh):
    in_specs = (
        P(None, ("patch", "level")),
        P(None, ("patch", "level"), None, None, None),
        P(("patch", "level"), None, None, None),
        P(("patch", "level"), None),
        P(("patch", "level")),
    )
    out_specs = P(None, ("patch", "level"))
    return jax.shard_map(
        per_device, mesh=mesh, in_specs=in_specs, out_specs=out_specs, check_vma=False
    )
```

```python
import functools

import jax
import jax.numpy as jnp
from jax import lax
from jax.experimental import pallas as pl
from jax.experimental.pallas import tpu as pltpu
from jax.sharding import PartitionSpec as P

ITERS = 3
CHAINS = 2
NEAR_TIES = ((1, 0, 0), (1, 1, 0))


coupling = 0.4


def exchange(block, axis, flip):
    route = [(i, i ^ flip) for i in range(lax.axis_size(axis))]
    return lax.ppermute(block, axis, route)


def exchange_next(block, axis):
    count = lax.axis_size(axis)
    route = []
    for i in range(1, count, 2):
        route += [(i, (i + 1) % count), ((i + 1) % count, i)]
    return lax.ppermute(block, axis, route)


def pair_product(own, partner, factor):
    both = jnp.concatenate([own, partner], axis=-1)
    weights = factor.reshape(2 * factor.shape[-2], factor.shape[-1])
    return jnp.dot(both, weights, preferred_element_type=jnp.float32)


def place(array):
    return pl.BlockSpec(memory_space=pltpu.SMEM if array.dtype == jnp.int32 else pltpu.VMEM)


def call(kernel, out_shape, operands, flops, scratch=()):
    size = sum(op.size * op.dtype.itemsize for op in operands)
    return pl.pallas_call(
        kernel,
        out_shape=out_shape,
        in_specs=[place(op) for op in operands],
        scratch_shapes=scratch,
        out_specs=jax.tree.map(place, out_shape),
        cost_estimate=pl.CostEstimate(flops=flops, bytes_accessed=size, transcendentals=0),
        compiler_params=pltpu.CompilerParams(vmem_limit_bytes=8 * 2**20),
    )(*operands)


def split_kernel(start, rows_ref, out_ref):
    blocks, _, width = out_ref.shape
    for b in range(blocks):
        out_ref[b] = rows_ref[:, (start + b) * width:(start + b + 1) * width]


def local_kernel(levels, start, z_ref, factor_ref, out_ref):
    blocks = z_ref.shape[0]
    mixed = [z_ref[b] for b in range(blocks)]
    for level in range(levels):
        mixed = [
            pair_product(
                mixed[b], mixed[b ^ (1 << level)], factor_ref[level, start + b]
            ).astype(jnp.bfloat16)
            for b in range(blocks)
        ]
    for b in range(blocks):
        out_ref[b] = mixed[b]


def level_kernel(level, start, own_ref, partner_ref, factor_ref, *refs):
    out_ref = refs[-1]
    for b in range(own_ref.shape[0]):
        out_ref[b] = pair_product(own_ref[b], partner_ref[b], factor_ref[level, start + b]).astype(
            jnp.bfloat16
        )


def near_kernel(start, index_ref, count_ref, *refs):
    pieces, near_ref, out_ref, window = refs[:-3], *refs[-3:]
    blocks = out_ref.shape[0]
    slots, width = near_ref.shape[1:3]
    unused = 0
    for piece in pieces:
        window[unused:unused + piece.shape[0]] = piece[...]
        unused += piece.shape[0]
    window[unused] = jnp.zeros(window.shape[1:], window.dtype)
    last = 2 * near_ref.shape[0]
    even = lax.axis_index("patch") % 2 == 0
    below, above = jnp.where(even, last, 0), jnp.where(even, -last, 0)

    def place_of(k, b):
        at = index_ref[k, b]
        shift = jnp.where(at < last // 2, below, jnp.where(at < last, 0, above))
        return jnp.where(k < count_ref[b], at + shift, unused)

    for b in range(start, start + blocks):
        taken = [window[place_of(k, b)] for k in range(slots)]
        out_ref[b - start] = jnp.dot(
            jnp.concatenate(taken, axis=-1),
            near_ref[b].reshape(slots * width, width),
            preferred_element_type=jnp.float32,
        )


def take_kernel(level, *refs):
    refs[-1][0] = refs[-2][level]


def last_kernel(level, start, own_ref, partner_ref, factor_ref, near_ref, source_ref, out_ref):
    for b in range(own_ref.shape[0]):
        mixed = pair_product(own_ref[b], partner_ref[b], factor_ref[level, start + b])
        mixed = mixed.astype(jnp.bfloat16).astype(jnp.float32)
        total = source_ref[b].astype(jnp.float32) - coupling * (mixed + near_ref[b])
        out_ref[b] = total.astype(jnp.bfloat16)


def stack_kernel(count, *refs):
    at = 0
    for part in refs[:count]:
        refs[-1][at:at + part.shape[0]] = part[...]
        at += part.shape[0]


def final_kernel(
    level, start, own_ref, partner_ref, factor_ref, near_ref, source_ref, before_ref, out_ref
):
    width = own_ref.shape[-1]
    for b in range(start):
        out_ref[:, b * width:(b + 1) * width] = before_ref[b]
    for b in range(own_ref.shape[0]):
        mixed = pair_product(own_ref[b], partner_ref[b], factor_ref[level, start + b])
        mixed = mixed.astype(jnp.bfloat16).astype(jnp.float32)
        total = source_ref[b].astype(jnp.float32) - coupling * (mixed + near_ref[b])
        at = (start + b) * width
        out_ref[:, at:at + width] = total.astype(jnp.bfloat16)


def per_device(right_side, level_pairs, near_blocks, near_index, near_count):
    rhs_count = right_side.shape[0]
    blocks, slots, width, _ = near_blocks.shape
    levels = level_pairs.shape[0]
    level_bits = lax.axis_size("level").bit_length() - 1
    patch_bits = lax.axis_size("patch").bit_length() - 1
    core = levels - level_bits - patch_bits
    half = blocks // CHAINS
    chains = range(CHAINS)
    piece = jax.ShapeDtypeStruct((half, rhs_count, width), jnp.bfloat16)
    whole = jax.ShapeDtypeStruct((blocks, rhs_count, width), jnp.bfloat16)
    near_shape = jax.ShapeDtypeStruct((half, rhs_count, width), jnp.float32)
    one_level = jax.ShapeDtypeStruct((1, *level_pairs.shape[1:]), jnp.bfloat16)
    flat = jax.ShapeDtypeStruct(right_side.shape, jnp.bfloat16)
    level_flops = 4 * half * rhs_count * width * width
    window_shape = pltpu.VMEM((3 * blocks + 1, rhs_count, width), jnp.bfloat16)

    rings = [
        (core + 1 + i, "level", 1 << (1 + i)) for i in range(0, level_bits - 1, 2)
    ] + [(core + level_bits + i, "patch", 1 << i) for i in range(0, patch_bits, 2)]
    early = level_pairs[:core + 1]
    factors = [(early, level) for level in range(core + 1)]
    factors += [(level_pairs, level) for level in range(core + 1, levels)]

    def sent(level, axis, flip, after):
        taken = call(functools.partial(take_kernel, level), one_level, (*after, level_pairs), 0)
        return exchange(taken, axis, flip)

    partner_factors = {
        level: exchange(level_pairs[level:level + 1], axis, flip) for level, axis, flip in rings[1:]
    }

    def product(kernel, c, own, partner, factor, *more, shape=piece):
        pairs, level = factor
        return call(
            functools.partial(kernel, level, c * half),
            shape,
            (own, partner, pairs, *more),
            level_flops,
        )

    source = [
        call(functools.partial(split_kernel, c * half), piece, (right_side,), 0) for c in chains
    ]
    current = list(source)
    for sweep in range(ITERS):
        mixed = [
            call(
                functools.partial(local_kernel, core, c * half),
                piece,
                (current[c], early),
                core * level_flops,
            )
            for c in chains
        ]
        def window_of(*after):
            joined = call(functools.partial(stack_kernel, CHAINS), whole, (*current, *after), 0)
            return exchange(joined, "patch", 1), joined, exchange_next(joined, "patch")

        def near_of(c):
            return call(
                functools.partial(near_kernel, c * half),
                near_shape,
                (near_index.T, near_count, *window, near_blocks),
                2 * half * slots * rhs_count * width * width,
                (window_shape,),
            )

        ties = {(2, 0, 0): near_blocks}
        if sweep > 0:
            ties = {}
            window = window_of()
            near = [near_of(c) for c in chains]
            ties[0, 1, 0] = window[2]
            for c in chains:
                ties[NEAR_TIES[c]] = near[c]
        for c in chains:
            partner = exchange(mixed[c], "level", 1)
            mixed[c] = product(level_kernel, c, mixed[c], partner, factors[core])
        for ring, (level, axis, flip) in enumerate(rings):
            for c in chains:
                partner = exchange(mixed[c], axis, flip)
                own = product(level_kernel, c, mixed[c], partner, factors[level])
                extra = [ties[ring, 0, c]] if (ring, 0, c) in ties else []
                more = [ties[ring, 1, c]] if (ring, 1, c) in ties else []
                if level in partner_factors:
                    theirs = product(
                        level_kernel, c, partner, mixed[c], (partner_factors[level], 0), *extra
                    )
                    partner = exchange(theirs, axis, 3 * flip)
                else:
                    partner = exchange(own, axis, 2 * flip)
                second = factors[level + 1]
                if ring == len(rings) - 1 and sweep == ITERS - 1 and c == CHAINS - 1:
                    mixed[c] = product(
                        final_kernel, c, own, partner, second, near[c], source[c], mixed[0],
                        shape=flat,
                    )
                elif ring == len(rings) - 1:
                    mixed[c] = product(last_kernel, c, own, partner, second, near[c], source[c])
                else:
                    mixed[c] = product(level_kernel, c, own, partner, second, *more)
            if sweep == 0 and ring == 1:
                window = window_of(mixed[0])
                near = [near_of(c) for c in chains]
            if level not in partner_factors:
                partner_factors[level] = sent(level, axis, flip, mixed)
        current = mixed
    return current[-1]


def solution(mesh):
    in_specs = (
        P(None, ("patch", "level")),
        P(None, ("patch", "level"), None, None, None),
        P(("patch", "level"), None, None, None),
        P(("patch", "level"), None),
        P(("patch", "level")),
    )
    out_specs = P(None, ("patch", "level"))
    return jax.shard_map(
        per_device, mesh=mesh, in_specs=in_specs, out_specs=out_specs, check_vma=False
    )
```
